32 devices in a mesh: fsdp: 16 (over z, y, core), tensor: 2 (over x).
Axes of the slice: x: 2, y: 2, z: 4, core: 2. Of those that a mesh axis runs over, the one named last changes fastest.
Arguments:
- tokens: bfloat16 [2, 8192, 1024], P(None, ('fsdp', 'tensor')), may hold values from -6 to 6
- doc_lengths: int32 [2, 16, 4], P(None, 'fsdp'), may hold values from 1 to 256, 512 in all within a row
- attn_gain: float32 [1024], replicated, may hold values from 0.1 to 1.9
- query_weight: bfloat16 [1024, 1024], P('fsdp', 'tensor'), may hold values from -0.1875 to 0.1875
- key_weight: bfloat16 [1024, 512], P('fsdp', 'tensor'), may hold values from -0.1875 to 0.1875
- value_weight: bfloat16 [1024, 512], P('fsdp', 'tensor'), may hold values from -0.1875 to 0.1875
- query_gain: float32 [64], replicated, may hold values from 0.1 to 1.9
- key_gain: float32 [64], replicated, may hold values from 0.1 to 1.9
- out_weight: bfloat16 [1024, 1024], P('tensor', 'fsdp'), may hold values from -1 to 1
- ffn_gain: float32 [1024], replicated, may hold values from 0.1 to 1.9
- gate_weight: bfloat16 [1024, 4608], P('fsdp', 'tensor'), may hold values from -0.1875 to 0.1875
- up_weight: bfloat16 [1024, 4608], P('fsdp', 'tensor'), may hold values from -0.1875 to 0.1875
- down_weight: bfloat16 [4608, 1024], P('tensor', 'fsdp'), may hold values from -0.1875 to 0.1875
- cotangent: bfloat16 [2, 8192, 1024], P(None, ('fsdp', 'tensor')), may hold values from -6 to 6
Outputs:
- block_out: bfloat16 [2, 8192, 1024], P(None, ('fsdp', 'tensor'))
- token_grad: float32 [2, 8192, 1024], P(None, ('fsdp', 'tensor'))
- attn_gain_grad: float32 [1024], replicated
- query_weight_grad: float32 [1024, 1024], P('fsdp', 'tensor')
- key_weight_grad: float32 [1024, 512], P('fsdp', 'tensor')
- value_weight_grad: float32 [1024, 512], P('fsdp', 'tensor')
- query_gain_grad: float32 [64], replicated
- key_gain_grad: float32 [64], replicated
- out_weight_grad: float32 [1024, 1024], P('tensor', 'fsdp')
- ffn_gain_grad: float32 [1024], replicated
- gate_weight_grad: float32 [1024, 4608], P('fsdp', 'tensor')
- up_weight_grad: float32 [1024, 4608], P('fsdp', 'tensor')
- down_weight_grad: float32 [4608, 1024], P('tensor', 'fsdp')
The draws below stay inside these ranges and needn't reach their ends.
Inputs may be any that keep to these rules, and one draw needn't show every extreme that they name: `doc_lengths`: each row of 4 document lengths sums to 512, and its longest document has exactly 256 tokens.
All inputs are finite; a program needn't handle non-finite values.
Results may differ from the reference program's by a relative error of at most 0.018.
Values may be sent and summed in bfloat16 or wider, within the bound.
A program may use at most 192 MiB of HBM per device.

```python
import math
import jax
import jax.numpy as jnp
import numpy as np
from jax import lax

D = 1024
H = 16
KV = 8
HD = 64
FF = 4608
SEQ = 512
MICRO = 2
DOCS = 4
TOKENS = 8192
N_FSDP = 16


def steps_of(rng, extent, pieces, least, largest):
    factor_of = 1.0
    for position, parts in pieces:
        steps = jax.random.uniform(jax.random.fold_in(jax.random.fold_in(rng, 6), position), (parts,), jnp.float32, least / len(pieces), largest / len(pieces))
        factor_of = factor_of * jnp.repeat(jnp.exp(steps), extent[position] // parts).reshape((-1,) + (1,) * (len(extent) - 1 - position))
    return factor_of


def profile(count, total, most, slope):
    loads = [(1 << 20) // math.isqrt(rank ** slope) + 1 for rank in range(2, count + 1)]
    rest, holding = total - most - (count - 1), [1] * (count - 1)
    while rest > 0:
        movable = [i for i in range(count - 1) if holding[i] < most]
        pool, budget = sum([loads[i] for i in movable]), rest
        for i in movable:
            extra = min(most - holding[i], max(1, budget * loads[i] // pool), rest)
            holding[i] = holding[i] + extra
            rest = rest - extra
    return np.array([most] + holding)


def uneven_parts(stream_key, amount, total, bound, slope):
    if amount == 2:
        one = jax.random.randint(stream_key, (), max(1, total - bound), min(bound, total - 1) + 1)
        return jnp.stack([one, total - one])
    lengths = jnp.asarray(profile(amount, total, bound, slope), jnp.int32)
    couples = (amount - 1) // 2
    giver, sink = lengths[1:1 + 2 * couples:2], lengths[2:2 + 2 * couples:2]
    slack = jnp.minimum(giver - 1, bound - sink)
    moved = jax.random.randint(jax.random.fold_in(stream_key, 1), (couples,), 0, 1 << 20) % (slack + 1)
    lengths = lengths.at[1:1 + 2 * couples:2].set(giver - moved).at[2:2 + 2 * couples:2].set(sink + moved)
    return lengths[jax.random.permutation(jax.random.fold_in(stream_key, 2), amount)]


def gaussian(rng, dims, spread, most, split=(), held_as=jnp.bfloat16):
    values = jax.random.normal(rng, dims, jnp.float32) * spread
    if len(split) > 0:
        values = steps_of(rng, dims, split, -0.22, 0.18) * values
    return jnp.clip(values, min=-most, max=most).astype(held_as)


def setup_inputs(seed: int = 0) -> dict:
    key_of = jax.random.split(jax.random.key(seed), 15)
    tokens = gaussian(key_of[0], (MICRO, TOKENS, D), 1.0, 6.0, ((1, 32),))
    doc_lengths = jax.vmap(lambda own: uneven_parts(own, DOCS, SEQ, SEQ // 2, 2))(jax.random.split(key_of[1], MICRO * N_FSDP)).reshape((MICRO, N_FSDP, DOCS)).astype(jnp.int32)
    attn_gain = jnp.clip(1.0 + 0.18 * jax.random.normal(key_of[2], (D,), jnp.float32), 0.1, 1.9)
    query_weight = gaussian(key_of[3], (D, H * HD), D ** -0.5, 0.1875, ((0, 16), (1, 2)))
    key_weight = gaussian(key_of[4], (D, KV * HD), D ** -0.5, 0.1875, ((0, 16), (1, 2)))
    value_weight = gaussian(key_of[5], (D, KV * HD), D ** -0.5, 0.1875, ((0, 16), (1, 2)))
    query_gain = jnp.clip(1.0 + 0.18 * jax.random.normal(key_of[6], (HD,), jnp.float32), 0.1, 1.9)
    key_gain = jnp.clip(1.0 + 0.18 * jax.random.normal(key_of[7], (HD,), jnp.float32), 0.1, 1.9)
    out_weight = gaussian(key_of[8], (H * HD, D), (H * HD // 32) ** -0.5, 1.0, ((0, 2), (1, 16)))
    ffn_gain = jnp.clip(1.0 + 0.18 * jax.random.normal(key_of[9], (D,), jnp.float32), 0.1, 1.9)
    gate_weight = gaussian(key_of[10], (D, FF), D ** -0.5, 0.1875, ((0, 16), (1, 2)))
    up_weight = gaussian(key_of[11], (D, FF), D ** -0.5, 0.1875, ((0, 16), (1, 2)))
    down_weight = gaussian(key_of[12], (FF, D), (FF // 4) ** -0.5, 0.1875, ((0, 2), (1, 16)))
    cotangent = gaussian(key_of[13], (MICRO, TOKENS, D), 1.0, 6.0, ((1, 32),))
    return dict(tokens=tokens, doc_lengths=doc_lengths, attn_gain=attn_gain, query_weight=query_weight, key_weight=key_weight, value_weight=value_weight, query_gain=query_gain, key_gain=key_gain, out_weight=out_weight, ffn_gain=ffn_gain, gate_weight=gate_weight, up_weight=up_weight, down_weight=down_weight, cotangent=cotangent)


@jax.custom_vjp
def low(v):
    return lax.optimization_barrier(v.astype(jnp.bfloat16)).astype(jnp.float32)

@jax.custom_vjp
def low_back(v):
    return v

def low_keep(v):
    return (low(v), None)

def low_pass(kept, grad):
    return (grad,)

def back_keep(v):
    return (v, None)

def back_low(kept, grad):
    return (low(grad),)
low.defvjp(low_keep, low_pass)
low_back.defvjp(back_keep, back_low)
EPSILON = 1e-05
ROPE_BASE = 1000000.0
MASKED = -1e+30

def matmul_high(left, right):
    return jnp.dot(left, right, precision=lax.Precision.HIGHEST, preferred_element_type=jnp.float32)

def rms_norm(values, gain_vec):
    return values * lax.rsqrt(lax.optimization_barrier(jnp.mean(values * values, axis=-1, keepdims=True)) + EPSILON) * gain_vec

def position_tables(doc_lens, row_count):
    lens_int = doc_lens.astype(jnp.int32)
    doc_ends = jnp.cumsum(lens_int).astype(jnp.int32)
    places = jnp.arange(row_count, dtype=jnp.int32)
    passed = places[:, None] >= doc_ends[None, :]
    segment = lax.optimization_barrier(jnp.sum(passed.astype(jnp.int32), axis=-1)).astype(jnp.int32)
    starts = lax.optimization_barrier(jnp.sum(jnp.where(passed, lens_int[None, :], 0), axis=-1)).astype(jnp.int32)
    offsets = (places - starts).astype(jnp.float32)
    return (segment, offsets)

def rotary_tables(offsets, head_dim):
    half_dim = head_dim // 2
    frequency = ROPE_BASE ** (-2.0 * jnp.arange(half_dim, dtype=jnp.float32) / head_dim)
    angles = offsets[:, None] * frequency[None, :]
    return (jnp.cos(angles)[:, None, :], jnp.sin(angles)[:, None, :])

def rotary(values, cosine, sine_part):
    half_dim = values.shape[-1] // 2
    first_half = values[..., :half_dim]
    second = values[..., half_dim:]
    return jnp.concatenate([first_half * cosine - second * sine_part, second * cosine + first_half * sine_part], axis=-1)

def seq_block(rows_in, doc_lens, params):
    attn_gain, query_weight, key_weight, value_weight, query_gain, key_gain, out_weight, ffn_gain, gate_weight, up_weight, down_weight = params
    row_count = rows_in.shape[0]
    segment, offsets = position_tables(doc_lens, row_count)
    cosine, sine_part = rotary_tables(offsets, HD)
    places = jnp.arange(row_count, dtype=jnp.int32)
    allowed = (segment[:, None] == segment[None, :]) & (places[None, :] <= places[:, None])
    normed = low(rms_norm(rows_in, attn_gain))
    query_proj = low_back(matmul_high(normed, query_weight))
    key_proj = low_back(matmul_high(normed, key_weight))
    value_proj = low_back(matmul_high(normed, value_weight))
    query = low(rotary(rms_norm(query_proj.reshape(row_count, H, HD), query_gain), cosine, sine_part))
    query = query.reshape(row_count, KV, H // KV, HD)
    key = low(rotary(rms_norm(key_proj.reshape(row_count, KV, HD), key_gain), cosine, sine_part))
    value = low(value_proj.reshape(row_count, KV, HD))
    scores = low_back(jnp.einsum('qngd,knd->ngqk', query, key, precision=lax.Precision.HIGHEST) / math.sqrt(HD))
    scores = jnp.where(allowed[None, None], scores, MASKED)
    attention = low(jax.nn.softmax(scores, axis=-1))
    mixed = jnp.einsum('ngqk,knd->qngd', attention, value, precision=lax.Precision.HIGHEST).reshape(row_count, H * HD)
    mixed = low(low_back(mixed))
    hidden_one = rows_in + low_back(matmul_high(mixed, out_weight))
    normed_two = low(rms_norm(hidden_one, ffn_gain))
    gate_act = low_back(matmul_high(normed_two, gate_weight))
    up_act = low_back(matmul_high(normed_two, up_weight))
    inner = low(jax.nn.silu(gate_act) * up_act)
    return hidden_one + low_back(matmul_high(inner, down_weight))

def reference(tokens, doc_lengths, attn_gain, query_weight, key_weight, value_weight, query_gain, key_gain, out_weight, ffn_gain, gate_weight, up_weight, down_weight, cotangent):
    params = tuple((weight_arr.astype(jnp.float32) for weight_arr in (attn_gain, query_weight, key_weight, value_weight, query_gain, key_gain, out_weight, ffn_gain, gate_weight, up_weight, down_weight)))
    rows_all = tokens.astype(jnp.float32)
    seq_lens = doc_lengths.reshape(MICRO * N_FSDP, DOCS)
    checked = jax.checkpoint(seq_block)

    def forward(all_rows, weights):
        slabs = all_rows.reshape(MICRO * N_FSDP, SEQ, D)

        def one_seq(slab_pair):
            return checked(slab_pair[0], slab_pair[1], weights)
        return lax.map(one_seq, (slabs, seq_lens)).reshape(MICRO, N_FSDP * SEQ, D)
    block_out, pullback = jax.vjp(forward, rows_all, params)
    token_grad, grad_sums = pullback(cotangent.astype(jnp.float32))
    return (block_out.astype(jnp.bfloat16), token_grad, grad_sums[0], grad_sums[1], grad_sums[2], grad_sums[3], grad_sums[4], grad_sums[5], grad_sums[6], grad_sums[7], grad_sums[8], grad_sums[9], grad_sums[10])
```

```python
import math

import jax
import jax.numpy as jnp
from jax import lax
from jax.sharding import PartitionSpec as P

D = 1024
H = 16
KV = 8
HD = 64
MICRO = 2


EPSILON = 1e-05
ROPE_BASE = 1000000.0
MASKED = -1e30


def position_tables(doc_lens, row_count):
    doc_ends = jnp.cumsum(doc_lens)
    places = jnp.arange(row_count, dtype=jnp.int32)
    passed = places[:, None] >= doc_ends[None, :]
    segment = jnp.sum(passed.astype(jnp.int32), axis=-1)
    starts = jnp.sum(jnp.where(passed, doc_lens[None, :], 0), axis=-1)
    offsets = (places - starts).astype(jnp.float32)
    return (segment, offsets)


def rotary_tables(offsets, head_dim):
    half_dim = head_dim // 2
    frequency = ROPE_BASE ** (-2.0 * jnp.arange(half_dim, dtype=jnp.float32) / head_dim)
    angles = offsets[:, None] * frequency[None, :]
    return (jnp.cos(angles)[:, None, :], jnp.sin(angles)[:, None, :])


def rotary(values, cosine, sine_part):
    half_dim = values.shape[-1] // 2
    first_half = values[..., :half_dim]
    second = values[..., half_dim:]
    return jnp.concatenate(
        [first_half * cosine - second * sine_part, second * cosine + first_half * sine_part],
        axis=-1,
    )


def rotary_back(grad_in, cosine, sine_part):
    half_dim = grad_in.shape[-1] // 2
    first_half = grad_in[..., :half_dim]
    second = grad_in[..., half_dim:]
    return jnp.concatenate(
        [first_half * cosine + second * sine_part, second * cosine - first_half * sine_part],
        axis=-1,
    )


def norm_stats(values):
    return lax.rsqrt(jnp.mean(values * values, axis=-1, keepdims=True) + EPSILON)


def norm_back(values, inverse, gain_vec, grad_in):
    scaled = grad_in * gain_vec
    back_vec = inverse * scaled - values * inverse * inverse * inverse * jnp.mean(
        values * scaled, axis=-1, keepdims=True
    )
    gain_part = jnp.sum(grad_in * values * inverse, axis=tuple(range(values.ndim - 1)))
    return (back_vec, gain_part)


def masked_scores(query_b, key_b, allowed, score_scale):
    scores = (
        jnp.einsum("qngd,knd->ngqk", query_b, key_b, preferred_element_type=jnp.float32)
        * score_scale
    )
    return jnp.where(allowed[None, None], scores, MASKED)


def fetch_attention(query_weight, key_weight, value_weight, out_weight):
    return (
        lax.all_gather(query_weight, "fsdp", axis=0, tiled=True),
        lax.all_gather(key_weight, "fsdp", axis=0, tiled=True),
        lax.all_gather(value_weight, "fsdp", axis=0, tiled=True),
        lax.all_gather(out_weight, "fsdp", axis=1, tiled=True),
    )


def fetch_feed(gate_weight, up_weight, down_weight):
    return (
        lax.all_gather(gate_weight, "fsdp", axis=0, tiled=True),
        lax.all_gather(up_weight, "fsdp", axis=0, tiled=True),
        lax.all_gather(down_weight, "fsdp", axis=1, tiled=True),
    )


def gather_rows(values):
    return lax.all_gather(values, "tensor", axis=0, tiled=True)


def scatter_rows(values):
    return lax.psum_scatter(values, "tensor", scatter_dimension=0, tiled=True)


def on_device(
    tokens,
    doc_lengths,
    attn_gain,
    query_weight,
    key_weight,
    value_weight,
    query_gain,
    key_gain,
    out_weight,
    ffn_gain,
    gate_weight,
    up_weight,
    down_weight,
    cotangent,
):
    head_local = query_weight.shape[1] // HD
    kv_local = key_weight.shape[1] // HD
    group_size = H // KV
    hidden_local = gate_weight.shape[1]
    score_scale = 1.0 / math.sqrt(HD)
    local_rows = tokens.shape[1]
    seq_rows = local_rows * lax.axis_size("tensor")
    places = jnp.arange(seq_rows, dtype=jnp.int32)
    query_acc = jnp.zeros((D, head_local * HD), jnp.float32)
    key_acc = jnp.zeros((D, kv_local * HD), jnp.float32)
    value_acc = jnp.zeros((D, kv_local * HD), jnp.float32)
    out_acc = jnp.zeros((head_local * HD, D), jnp.float32)
    gate_acc = jnp.zeros((D, hidden_local), jnp.float32)
    up_acc = jnp.zeros((D, hidden_local), jnp.float32)
    down_acc = jnp.zeros((hidden_local, D), jnp.float32)
    attn_part = jnp.zeros((D,), jnp.float32)
    ffn_part = jnp.zeros((D,), jnp.float32)
    query_part = jnp.zeros((HD,), jnp.float32)
    key_part = jnp.zeros((HD,), jnp.float32)
    outputs = []
    token_grads = []
    for micro_step in range(MICRO):
        attn_set = fetch_attention(query_weight, key_weight, value_weight, out_weight)
        feed_set = fetch_feed(gate_weight, up_weight, down_weight)
        query_full, key_full, value_full, out_full = attn_set
        gate_full, up_full, down_full = feed_set
        segment, offsets = position_tables(doc_lengths[micro_step, 0], seq_rows)
        cosine, sine_part = rotary_tables(offsets, HD)
        allowed = (segment[:, None] == segment[None, :]) & (places[None, :] <= places[:, None])
        rows_in = tokens[micro_step].astype(jnp.float32)
        inverse_one = norm_stats(rows_in)
        normed_b = (rows_in * inverse_one * attn_gain).astype(jnp.bfloat16)
        gathered = gather_rows(normed_b)
        query_proj = jnp.dot(gathered, query_full, preferred_element_type=jnp.float32)
        key_proj = jnp.dot(gathered, key_full, preferred_element_type=jnp.float32)
        value_proj = jnp.dot(gathered, value_full, preferred_element_type=jnp.float32)
        query_heads = query_proj.reshape(seq_rows, head_local, HD)
        inverse_q = norm_stats(query_heads)
        query_b = rotary(query_heads * inverse_q * query_gain, cosine, sine_part).astype(
            jnp.bfloat16
        )
        query_b = query_b.reshape(seq_rows, kv_local, group_size, HD)
        key_heads = key_proj.reshape(seq_rows, kv_local, HD)
        inverse_k = norm_stats(key_heads)
        key_b = rotary(key_heads * inverse_k * key_gain, cosine, sine_part).astype(jnp.bfloat16)
        value_b = value_proj.reshape(seq_rows, kv_local, HD).astype(jnp.bfloat16)
        scores = masked_scores(query_b, key_b, allowed, score_scale)
        row_max = jnp.max(scores, axis=-1, keepdims=True)
        log_total = row_max + jnp.log(jnp.sum(jnp.exp(scores - row_max), axis=-1, keepdims=True))
        attention_b = jnp.exp(scores - log_total).astype(jnp.bfloat16)
        mixed_b = jnp.einsum(
            "ngqk,knd->qngd", attention_b, value_b, preferred_element_type=jnp.float32
        )
        mixed_b = mixed_b.reshape(seq_rows, head_local * HD).astype(jnp.bfloat16)
        attn_terms = jnp.dot(mixed_b, out_full, preferred_element_type=jnp.float32)
        hidden_one = rows_in + scatter_rows(attn_terms)
        inverse_two = norm_stats(hidden_one)
        normed_two = (hidden_one * inverse_two * ffn_gain).astype(jnp.bfloat16)
        gathered_two = gather_rows(normed_two)
        gate_act = jnp.dot(gathered_two, gate_full, preferred_element_type=jnp.float32)
        up_act = jnp.dot(gathered_two, up_full, preferred_element_type=jnp.float32)
        inner_b = (jax.nn.silu(gate_act) * up_act).astype(jnp.bfloat16)
        ffn_out = scatter_rows(jnp.dot(inner_b, down_full, preferred_element_type=jnp.float32))
        outputs.append((hidden_one + ffn_out).astype(jnp.bfloat16))
        query_full, key_full, value_full, out_full = fetch_attention(
            query_weight, key_weight, value_weight, out_weight
        )
        gate_full, up_full, down_full = fetch_feed(gate_weight, up_weight, down_weight)
        grad_out = cotangent[micro_step].astype(jnp.float32)
        grad_ffn = gather_rows(grad_out.astype(jnp.bfloat16))
        grad_inner = jnp.dot(grad_ffn, down_full.T, preferred_element_type=jnp.float32)
        down_acc = down_acc + jnp.dot(inner_b.T, grad_ffn, preferred_element_type=jnp.float32)
        sig_gate = jax.nn.sigmoid(gate_act)
        grad_gate = (grad_inner * up_act * sig_gate * (1.0 + gate_act * (1.0 - sig_gate))).astype(
            jnp.bfloat16
        )
        grad_up = (grad_inner * gate_act * sig_gate).astype(jnp.bfloat16)
        gate_acc = gate_acc + jnp.dot(gathered_two.T, grad_gate, preferred_element_type=jnp.float32)
        up_acc = up_acc + jnp.dot(gathered_two.T, grad_up, preferred_element_type=jnp.float32)
        grad_normed_two = scatter_rows(
            jnp.dot(grad_gate, gate_full.T, preferred_element_type=jnp.float32)
            + jnp.dot(grad_up, up_full.T, preferred_element_type=jnp.float32)
        )
        back_two, ffn_piece = norm_back(hidden_one, inverse_two, ffn_gain, grad_normed_two)
        ffn_part = ffn_part + ffn_piece
        grad_hidden = grad_out + back_two
        grad_attn = gather_rows(grad_hidden.astype(jnp.bfloat16))
        out_acc = out_acc + jnp.dot(mixed_b.T, grad_attn, preferred_element_type=jnp.float32)
        grad_mixed = jnp.dot(grad_attn, out_full.T, preferred_element_type=jnp.float32).astype(
            jnp.bfloat16
        )
        grad_mixed = grad_mixed.reshape(seq_rows, kv_local, group_size, HD)
        scores = masked_scores(query_b, key_b, allowed, score_scale)
        attention = jnp.exp(scores - log_total)
        attention_b = attention.astype(jnp.bfloat16)
        grad_value = jnp.einsum(
            "ngqk,qngd->knd", attention_b, grad_mixed, preferred_element_type=jnp.float32
        )
        grad_attention = jnp.einsum(
            "qngd,knd->ngqk", grad_mixed, value_b, preferred_element_type=jnp.float32
        )
        grad_scores = attention * (
            grad_attention - jnp.sum(attention * grad_attention, axis=-1, keepdims=True)
        )
        grad_scores = grad_scores.astype(jnp.bfloat16)
        grad_query = (
            jnp.einsum("ngqk,knd->qngd", grad_scores, key_b, preferred_element_type=jnp.float32)
            * score_scale
        )
        grad_key = (
            jnp.einsum("ngqk,qngd->knd", grad_scores, query_b, preferred_element_type=jnp.float32)
            * score_scale
        )
        grad_qrot = rotary_back(grad_query.reshape(seq_rows, head_local, HD), cosine, sine_part)
        back_query, query_piece = norm_back(query_heads, inverse_q, query_gain, grad_qrot)
        grad_krot = rotary_back(grad_key, cosine, sine_part)
        back_key, key_piece = norm_back(key_heads, inverse_k, key_gain, grad_krot)
        query_part = query_part + query_piece
        key_part = key_part + key_piece
        grad_query_proj = back_query.reshape(seq_rows, head_local * HD).astype(jnp.bfloat16)
        grad_key_proj = back_key.reshape(seq_rows, kv_local * HD).astype(jnp.bfloat16)
        grad_value_proj = grad_value.reshape(seq_rows, kv_local * HD).astype(jnp.bfloat16)
        query_acc = query_acc + jnp.dot(
            gathered.T, grad_query_proj, preferred_element_type=jnp.float32
        )
        key_acc = key_acc + jnp.dot(gathered.T, grad_key_proj, preferred_element_type=jnp.float32)
        value_acc = value_acc + jnp.dot(
            gathered.T, grad_value_proj, preferred_element_type=jnp.float32
        )
        grad_normed = jnp.dot(grad_query_proj, query_full.T, preferred_element_type=jnp.float32)
        grad_normed = grad_normed + jnp.dot(
            grad_key_proj, key_full.T, preferred_element_type=jnp.float32
        )
        grad_normed = grad_normed + jnp.dot(
            grad_value_proj, value_full.T, preferred_element_type=jnp.float32
        )
        grad_normed = scatter_rows(grad_normed)
        back_one, attn_piece = norm_back(rows_in, inverse_one, attn_gain, grad_normed)
        attn_part = attn_part + attn_piece
        token_grads.append(grad_hidden + back_one)
    query_grad, key_grad, value_grad, out_grad, gate_grad, up_grad, down_grad = (
        lax.psum_scatter(
            query_acc.astype(jnp.bfloat16), "fsdp", scatter_dimension=0, tiled=True
        ).astype(jnp.float32),
        lax.psum_scatter(
            key_acc.astype(jnp.bfloat16), "fsdp", scatter_dimension=0, tiled=True
        ).astype(jnp.float32),
        lax.psum_scatter(
            value_acc.astype(jnp.bfloat16), "fsdp", scatter_dimension=0, tiled=True
        ).astype(jnp.float32),
        lax.psum_scatter(
            out_acc.astype(jnp.bfloat16), "fsdp", scatter_dimension=1, tiled=True
        ).astype(jnp.float32),
        lax.psum_scatter(
            gate_acc.astype(jnp.bfloat16), "fsdp", scatter_dimension=0, tiled=True
        ).astype(jnp.float32),
        lax.psum_scatter(
            up_acc.astype(jnp.bfloat16), "fsdp", scatter_dimension=0, tiled=True
        ).astype(jnp.float32),
        lax.psum_scatter(
            down_acc.astype(jnp.bfloat16), "fsdp", scatter_dimension=1, tiled=True
        ).astype(jnp.float32),
    )
    attn_total, query_total, key_total, ffn_total = lax.psum(
        (attn_part, query_part, key_part, ffn_part), ("fsdp", "tensor")
    )
    return (
        jnp.stack(outputs),
        jnp.stack(token_grads),
        attn_total,
        query_grad,
        key_grad,
        value_grad,
        query_total,
        key_total,
        out_grad,
        ffn_total,
        gate_grad,
        up_grad,
        down_grad,
    )


def swap_tensor(values):
    return lax.ppermute(values, "tensor", [(0, 1), (1, 0)])


def sequence_of(values, side):
    own = lax.dynamic_index_in_dim(values, side, 0, keepdims=False)
    other = swap_tensor(lax.dynamic_index_in_dim(values, 1 - side, 0, keepdims=False))
    first = jnp.where(side == 0, own, other)
    return jnp.concatenate([first, jnp.where(side == 0, other, own)], axis=0)


def rows_of(values, side, wire):
    halves = values.reshape((2, values.shape[0] // 2) + values.shape[1:])
    own = lax.dynamic_index_in_dim(halves, side, 0, keepdims=False)
    away = lax.dynamic_index_in_dim(halves, 1 - side, 0, keepdims=False)
    other = swap_tensor(away.astype(wire)).astype(values.dtype)
    return jnp.stack([jnp.where(side == 0, own, other), jnp.where(side == 0, other, own)])


def links():
    steps, distance = [("tensor", 1)], lax.axis_size("fsdp") // 2
    while distance:
        steps.append(("fsdp", distance))
        distance //= 2
    return steps


def exchange(values, link):
    name, distance = link
    pairs = [(i, i ^ distance) for i in range(lax.axis_size(name))]
    return lax.ppermute(values, name, pairs)


def total_of(values):
    for link in links():
        values = values + exchange(values, link)
    return values


def gather_steps(piece, order, steps):
    for step in order:
        other = exchange(piece, steps[step])
        piece = jnp.concatenate([piece, other], axis=step - 1 if step else piece.ndim - 1)
    return piece


def scatter_steps(values, order, steps):
    for step in order:
        axis = step - 1 if step else values.ndim - 1
        kept, sent = jnp.split(values, 2, axis=axis)
        other = exchange(sent, steps[step])
        values = (kept.astype(jnp.float32) + other.astype(jnp.float32)).astype(values.dtype)
    return values


def opened(weight, steps):
    return weight.reshape((1,) * (len(steps) - 1) + weight.shape)


def own_order(values, fsdp_index, blocks):
    grid = values.reshape(blocks, -1)
    return jnp.take(grid, jnp.arange(blocks) ^ fsdp_index, axis=0).reshape(values.shape)


def times(left, right):
    return jnp.dot(left, right, preferred_element_type=jnp.float32)


def times_t(left, right):
    return lax.dot_general(
        left, right, (((1,), (1,)), ((), ())), preferred_element_type=jnp.float32
    )


def rows_summed(left, right):
    return lax.dot_general(
        left, right, (((0,), (0,)), ((), ())), preferred_element_type=jnp.float32
    ).astype(jnp.bfloat16)


def whole_sequence(
    tokens,
    doc_lengths,
    attn_gain,
    query_weight,
    key_weight,
    value_weight,
    query_gain,
    key_gain,
    out_weight,
    ffn_gain,
    gate_weight,
    up_weight,
    down_weight,
    cotangent,
):
    side = lax.axis_index("tensor")
    blocks = lax.axis_size("fsdp")
    place = lax.axis_index("fsdp")
    q_cols = query_weight.shape[1]
    k_cols = key_weight.shape[1]
    group_size = H // KV
    score_scale = 1.0 / math.sqrt(HD)
    steps = links()
    last = len(steps) - 1
    far = list(range(1, last - 1))
    orders = (
        far + [last - 1, 0],
        far + [0, last - 1],
        [0, last - 1] + far,
    )
    qkv_local = jnp.concatenate([query_weight, key_weight, value_weight], axis=1)
    rows_own = sequence_of(tokens, side)
    qkv_part = gather_steps(opened(qkv_local, steps), orders[0], steps)
    out_part = gather_steps(opened(out_weight.T, steps), orders[1], steps)
    qkv_part, out_part, gate_local, up_local, down_local, cot_local = lax.optimization_barrier(
        (qkv_part, out_part, gate_weight, up_weight, down_weight, cotangent)
    )
    qkv_full = gather_steps(qkv_part, [last], steps).reshape(D, -1)
    out_full = gather_steps(out_part, [last], steps).reshape(D, -1)
    cot_own = sequence_of(cot_local, side)
    gate_full, up_full, down_full = (
        gather_steps(opened(weight, steps), order + [last], steps).reshape(D, -1)
        for weight, order in zip((gate_local, up_local, down_local.T), orders)
    )
    features = jnp.arange(D)
    block_rows = D // blocks
    moved = ((features // block_rows) ^ place) * block_rows + features % block_rows
    order_mat = (moved[:, None] == features[None, :]).astype(jnp.bfloat16)
    rows_b = times(rows_own, order_mat).astype(jnp.bfloat16)
    cot_b = times(cot_own, order_mat).astype(jnp.bfloat16)
    attn_gain = own_order(attn_gain, place, blocks)
    ffn_gain = own_order(ffn_gain, place, blocks)
    seq_rows = rows_b.shape[0]
    lengths = lax.dynamic_index_in_dim(doc_lengths, side, 0, keepdims=False)[0]
    segment, offsets = position_tables(lengths, seq_rows)
    places = jnp.arange(seq_rows, dtype=jnp.int32)
    cosine, sine_part = rotary_tables(offsets, HD)
    allowed = (segment[:, None] == segment[None, :]) & (places[None, :] <= places[:, None])

    rows_in = rows_b.astype(jnp.float32)
    inverse_one = norm_stats(rows_in)
    normed_b = (rows_in * inverse_one * attn_gain).astype(jnp.bfloat16)
    v_at, one = q_cols + k_cols, q_cols + 2 * k_cols
    projected = times(normed_b, qkv_full)
    halves = (projected[:, :one], projected[:, one:])
    query_proj = jnp.concatenate([p[:, :q_cols] for p in halves], axis=1)
    key_proj = jnp.concatenate([p[:, q_cols:v_at] for p in halves], axis=1)
    value_proj = jnp.concatenate([p[:, v_at:] for p in halves], axis=1)
    query_heads = query_proj.reshape(seq_rows, H, HD)
    inverse_q = norm_stats(query_heads)
    query_b = rotary(query_heads * inverse_q * query_gain, cosine, sine_part).astype(jnp.bfloat16)
    query_b = query_b.reshape(seq_rows, KV, group_size, HD)
    key_heads = key_proj.reshape(seq_rows, KV, HD)
    inverse_k = norm_stats(key_heads)
    key_b = rotary(key_heads * inverse_k * key_gain, cosine, sine_part).astype(jnp.bfloat16)
    value_b = value_proj.reshape(seq_rows, KV, HD).astype(jnp.bfloat16)
    scores = masked_scores(query_b, key_b, allowed, score_scale)
    row_max = jnp.max(scores, axis=-1, keepdims=True)
    log_total = row_max + jnp.log(jnp.sum(jnp.exp(scores - row_max), axis=-1, keepdims=True))
    attention = jnp.exp(scores - log_total)
    attention_b = attention.astype(jnp.bfloat16)
    mixed_b = jnp.einsum("ngqk,knd->qngd", attention_b, value_b, preferred_element_type=jnp.float32)
    mixed_b = mixed_b.reshape(seq_rows, H * HD).astype(jnp.bfloat16)
    hidden_one = rows_in + times_t(mixed_b, out_full)
    inverse_two = norm_stats(hidden_one)
    normed_two = (hidden_one * inverse_two * ffn_gain).astype(jnp.bfloat16)

    grad_out = cot_b.astype(jnp.float32)
    gate_act = times(normed_two, gate_full)
    up_act = times(normed_two, up_full)
    sig_gate = jax.nn.sigmoid(gate_act)
    inner_b = (gate_act * sig_gate * up_act).astype(jnp.bfloat16)
    grad_inner = times(cot_b, down_full)
    grad_gate = (grad_inner * up_act * sig_gate * (1.0 + gate_act * (1.0 - sig_gate))).astype(
        jnp.bfloat16
    )
    grad_up = (grad_inner * gate_act * sig_gate).astype(jnp.bfloat16)
    block_out = (hidden_one + times_t(inner_b, down_full)).astype(jnp.bfloat16)
    block_out = times(block_out, order_mat).astype(jnp.bfloat16)
    outputs = rows_of(block_out, side, jnp.bfloat16)
    wide = (blocks.bit_length() - 1) * (2,) + (block_rows, -1)

    def scatter_grad(grad, order):
        order = [last] + order[::-1]
        grad = scatter_steps(grad.reshape(wide), order, steps)
        return grad.reshape(block_rows, -1).astype(jnp.float32)

    down_grad = scatter_grad(rows_summed(cot_b, inner_b), orders[2])
    gate_grad = scatter_grad(rows_summed(normed_two, grad_gate), orders[0])
    up_grad = scatter_grad(rows_summed(normed_two, grad_up), orders[1])
    grad_normed_two = times_t(grad_gate, gate_full) + times_t(grad_up, up_full)

    back_two, ffn_part = norm_back(hidden_one, inverse_two, ffn_gain, grad_normed_two)
    grad_hidden = grad_out + back_two
    grad_attn = grad_hidden.astype(jnp.bfloat16)
    out_grad = scatter_grad(rows_summed(grad_attn, mixed_b), orders[1])
    grad_mixed = times(grad_attn, out_full).astype(jnp.bfloat16)
    grad_mixed = grad_mixed.reshape(seq_rows, KV, group_size, HD)
    grad_value = jnp.einsum(
        "ngqk,qngd->knd", attention_b, grad_mixed, preferred_element_type=jnp.float32
    )
    grad_attention = jnp.einsum(
        "qngd,knd->ngqk", grad_mixed, value_b, preferred_element_type=jnp.float32
    )
    grad_scores = attention * (
        grad_attention - jnp.sum(attention * grad_attention, axis=-1, keepdims=True)
    )
    grad_scores = grad_scores.astype(jnp.bfloat16)
    grad_query = (
        jnp.einsum("ngqk,knd->qngd", grad_scores, key_b, preferred_element_type=jnp.float32)
        * score_scale
    )
    grad_key = (
        jnp.einsum("ngqk,qngd->knd", grad_scores, query_b, preferred_element_type=jnp.float32)
        * score_scale
    )
    grad_qrot = rotary_back(grad_query.reshape(seq_rows, H, HD), cosine, sine_part)
    back_query, query_part = norm_back(query_heads, inverse_q, query_gain, grad_qrot)
    grad_krot = rotary_back(grad_key, cosine, sine_part)
    back_key, key_part = norm_back(key_heads, inverse_k, key_gain, grad_krot)
    grad_q = back_query.reshape(seq_rows, H * HD).astype(jnp.bfloat16)
    grad_k = back_key.reshape(seq_rows, KV * HD).astype(jnp.bfloat16)
    grad_v = grad_value.reshape(seq_rows, KV * HD).astype(jnp.bfloat16)
    grad_qkv = jnp.concatenate(
        [
            grad_q[:, :q_cols], grad_k[:, :k_cols], grad_v[:, :k_cols],
            grad_q[:, q_cols:], grad_k[:, k_cols:], grad_v[:, k_cols:],
        ],
        axis=1,
    )
    qkv_grad = scatter_grad(rows_summed(normed_b, grad_qkv), orders[0])
    grad_normed = times_t(grad_qkv, qkv_full)
    back_one, attn_part = norm_back(rows_in, inverse_one, attn_gain, grad_normed)
    token_grad = grad_hidden + back_one
    high = token_grad.astype(jnp.bfloat16)
    low = (token_grad - high.astype(jnp.float32)).astype(jnp.bfloat16)
    token_grad = times(high, order_mat) + times(low, order_mat)
    token_grad = rows_of(token_grad, side, jnp.bfloat16)
    gain_parts = [
        own_order(attn_part, place, blocks), own_order(ffn_part, place, blocks),
        query_part, key_part,
    ]
    gain_total = total_of(jnp.concatenate(gain_parts))
    return (
        outputs,
        token_grad,
        gain_total[:D],
        qkv_grad[:, :q_cols],
        qkv_grad[:, q_cols:v_at],
        qkv_grad[:, v_at:],
        gain_total[2 * D : 2 * D + HD],
        gain_total[2 * D + HD :],
        out_grad.T,
        gain_total[D : 2 * D],
        gate_grad,
        up_grad,
        down_grad.T,
    )


def solution(mesh):
    fsdp, tensor = mesh.shape["fsdp"], mesh.shape["tensor"]
    run = on_device
    if tensor == MICRO == 2 and fsdp >= 8 and fsdp & (fsdp - 1) == 0:
        run = whole_sequence
    in_specs = (
        P(None, ("fsdp", "tensor"), None),
        P(None, "fsdp", None),
        P(),
        P("fsdp", "tensor"),
        P("fsdp", "tensor"),
        P("fsdp", "tensor"),
        P(),
        P(),
        P("tensor", "fsdp"),
        P(),
        P("fsdp", "tensor"),
        P("fsdp", "tensor"),
        P("tensor", "fsdp"),
        P(None, ("fsdp", "tensor"), None),
    )
    out_specs = (
        P(None, ("fsdp", "tensor"), None),
        P(None, ("fsdp", "tensor"), None),
        P(),
        P("fsdp", "tensor"),
        P("fsdp", "tensor"),
        P("fsdp", "tensor"),
        P(),
        P(),
        P("tensor", "fsdp"),
        P(),
        P("fsdp", "tensor"),
        P("fsdp", "tensor"),
        P("tensor", "fsdp"),
    )
    return jax.shard_map(
        run, mesh=mesh, in_specs=in_specs, out_specs=out_specs, check_vma=False
    )
```

```python
import math

import jax
import jax.numpy as jnp
from jax import lax
from jax.sharding import PartitionSpec as P

D = 1024
H = 16
KV = 8
HD = 64
MICRO = 2


EPSILON = 1e-05
ROPE_BASE = 1000000.0
MASKED = -1e30


def position_tables(doc_lens, row_count):
    doc_ends = jnp.cumsum(doc_lens)
    places = jnp.arange(row_count, dtype=jnp.int32)
    passed = places[:, None] >= doc_ends[None, :]
    segment = jnp.sum(passed.astype(jnp.int32), axis=-1)
    starts = jnp.sum(jnp.where(passed, doc_lens[None, :], 0), axis=-1)
    offsets = (places - starts).astype(jnp.float32)
    return (segment, offsets)


def rotary_tables(offsets, head_dim):
    half_dim = head_dim // 2
    frequency = ROPE_BASE ** (-2.0 * jnp.arange(half_dim, dtype=jnp.float32) / head_dim)
    angles = offsets[:, None] * frequency[None, :]
    return (jnp.cos(angles)[:, None, :], jnp.sin(angles)[:, None, :])


def rotary(values, cosine, sine_part):
    half_dim = values.shape[-1] // 2
    first_half = values[..., :half_dim]
    second = values[..., half_dim:]
    return jnp.concatenate(
        [first_half * cosine - second * sine_part, second * cosine + first_half * sine_part],
        axis=-1,
    )


def rotary_back(grad_in, cosine, sine_part):
    half_dim = grad_in.shape[-1] // 2
    first_half = grad_in[..., :half_dim]
    second = grad_in[..., half_dim:]
    return jnp.concatenate(
        [first_half * cosine + second * sine_part, second * cosine - first_half * sine_part],
        axis=-1,
    )


def norm_stats(values):
    return lax.rsqrt(jnp.mean(values * values, axis=-1, keepdims=True) + EPSILON)


def norm_back(values, inverse, gain_vec, grad_in):
    scaled = grad_in * gain_vec
    back_vec = inverse * scaled - values * inverse * inverse * inverse * jnp.mean(
        values * scaled, axis=-1, keepdims=True
    )
    gain_part = jnp.sum(grad_in * values * inverse, axis=tuple(range(values.ndim - 1)))
    return (back_vec, gain_part)


def masked_scores(query_b, key_b, allowed, score_scale):
    scores = (
        jnp.einsum("qngd,knd->ngqk", query_b, key_b, preferred_element_type=jnp.float32)
        * score_scale
    )
    return jnp.where(allowed[None, None], scores, MASKED)


def fetch_attention(query_weight, key_weight, value_weight, out_weight):
    return (
        lax.all_gather(query_weight, "fsdp", axis=0, tiled=True),
        lax.all_gather(key_weight, "fsdp", axis=0, tiled=True),
        lax.all_gather(value_weight, "fsdp", axis=0, tiled=True),
        lax.all_gather(out_weight, "fsdp", axis=1, tiled=True),
    )


def fetch_feed(gate_weight, up_weight, down_weight):
    return (
        lax.all_gather(gate_weight, "fsdp", axis=0, tiled=True),
        lax.all_gather(up_weight, "fsdp", axis=0, tiled=True),
        lax.all_gather(down_weight, "fsdp", axis=1, tiled=True),
    )


def gather_rows(values):
    return lax.all_gather(values, "tensor", axis=0, tiled=True)


def scatter_rows(values):
    return lax.psum_scatter(values, "tensor", scatter_dimension=0, tiled=True)


def on_device(
    tokens,
    doc_lengths,
    attn_gain,
    query_weight,
    key_weight,
    value_weight,
    query_gain,
    key_gain,
    out_weight,
    ffn_gain,
    gate_weight,
    up_weight,
    down_weight,
    cotangent,
):
    head_local = query_weight.shape[1] // HD
    kv_local = key_weight.shape[1] // HD
    group_size = H // KV
    hidden_local = gate_weight.shape[1]
    score_scale = 1.0 / math.sqrt(HD)
    local_rows = tokens.shape[1]
    seq_rows = local_rows * lax.axis_size("tensor")
    places = jnp.arange(seq_rows, dtype=jnp.int32)
    query_acc = jnp.zeros((D, head_local * HD), jnp.float32)
    key_acc = jnp.zeros((D, kv_local * HD), jnp.float32)
    value_acc = jnp.zeros((D, kv_local * HD), jnp.float32)
    out_acc = jnp.zeros((head_local * HD, D), jnp.float32)
    gate_acc = jnp.zeros((D, hidden_local), jnp.float32)
    up_acc = jnp.zeros((D, hidden_local), jnp.float32)
    down_acc = jnp.zeros((hidden_local, D), jnp.float32)
    attn_part = jnp.zeros((D,), jnp.float32)
    ffn_part = jnp.zeros((D,), jnp.float32)
    query_part = jnp.zeros((HD,), jnp.float32)
    key_part = jnp.zeros((HD,), jnp.float32)
    outputs = []
    token_grads = []
    for micro_step in range(MICRO):
        attn_set = fetch_attention(query_weight, key_weight, value_weight, out_weight)
        feed_set = fetch_feed(gate_weight, up_weight, down_weight)
        query_full, key_full, value_full, out_full = attn_set
        gate_full, up_full, down_full = feed_set
        segment, offsets = position_tables(doc_lengths[micro_step, 0], seq_rows)
        cosine, sine_part = rotary_tables(offsets, HD)
        allowed = (segment[:, None] == segment[None, :]) & (places[None, :] <= places[:, None])
        rows_in = tokens[micro_step].astype(jnp.float32)
        inverse_one = norm_stats(rows_in)
        normed_b = (rows_in * inverse_one * attn_gain).astype(jnp.bfloat16)
        gathered = gather_rows(normed_b)
        query_proj = jnp.dot(gathered, query_full, preferred_element_type=jnp.float32)
        key_proj = jnp.dot(gathered, key_full, preferred_element_type=jnp.float32)
        value_proj = jnp.dot(gathered, value_full, preferred_element_type=jnp.float32)
        query_heads = query_proj.reshape(seq_rows, head_local, HD)
        inverse_q = norm_stats(query_heads)
        query_b = rotary(query_heads * inverse_q * query_gain, cosine, sine_part).astype(
            jnp.bfloat16
        )
        query_b = query_b.reshape(seq_rows, kv_local, group_size, HD)
        key_heads = key_proj.reshape(seq_rows, kv_local, HD)
        inverse_k = norm_stats(key_heads)
        key_b = rotary(key_heads * inverse_k * key_gain, cosine, sine_part).astype(jnp.bfloat16)
        value_b = value_proj.reshape(seq_rows, kv_local, HD).astype(jnp.bfloat16)
        scores = masked_scores(query_b, key_b, allowed, score_scale)
        row_max = jnp.max(scores, axis=-1, keepdims=True)
        log_total = row_max + jnp.log(jnp.sum(jnp.exp(scores - row_max), axis=-1, keepdims=True))
        attention_b = jnp.exp(scores - log_total).astype(jnp.bfloat16)
        mixed_b = jnp.einsum(
            "ngqk,knd->qngd", attention_b, value_b, preferred_element_type=jnp.float32
        )
        mixed_b = mixed_b.reshape(seq_rows, head_local * HD).astype(jnp.bfloat16)
        attn_terms = jnp.dot(mixed_b, out_full, preferred_element_type=jnp.float32)
        hidden_one = rows_in + scatter_rows(attn_terms)
        inverse_two = norm_stats(hidden_one)
        normed_two = (hidden_one * inverse_two * ffn_gain).astype(jnp.bfloat16)
        gathered_two = gather_rows(normed_two)
        gate_act = jnp.dot(gathered_two, gate_full, preferred_element_type=jnp.float32)
        up_act = jnp.dot(gathered_two, up_full, preferred_element_type=jnp.float32)
        inner_b = (jax.nn.silu(gate_act) * up_act).astype(jnp.bfloat16)
        ffn_out = scatter_rows(jnp.dot(inner_b, down_full, preferred_element_type=jnp.float32))
        outputs.append((hidden_one + ffn_out).astype(jnp.bfloat16))
        query_full, key_full, value_full, out_full = fetch_attention(
            query_weight, key_weight, value_weight, out_weight
        )
        gate_full, up_full, down_full = fetch_feed(gate_weight, up_weight, down_weight)
        grad_out = cotangent[micro_step].astype(jnp.float32)
        grad_ffn = gather_rows(grad_out.astype(jnp.bfloat16))
        grad_inner = jnp.dot(grad_ffn, down_full.T, preferred_element_type=jnp.float32)
        down_acc = down_acc + jnp.dot(inner_b.T, grad_ffn, preferred_element_type=jnp.float32)
        sig_gate = jax.nn.sigmoid(gate_act)
        grad_gate = (grad_inner * up_act * sig_gate * (1.0 + gate_act * (1.0 - sig_gate))).astype(
            jnp.bfloat16
        )
        grad_up = (grad_inner * gate_act * sig_gate).astype(jnp.bfloat16)
        gate_acc = gate_acc + jnp.dot(gathered_two.T, grad_gate, preferred_element_type=jnp.float32)
        up_acc = up_acc + jnp.dot(gathered_two.T, grad_up, preferred_element_type=jnp.float32)
        grad_normed_two = scatter_rows(
            jnp.dot(grad_gate, gate_full.T, preferred_element_type=jnp.float32)
            + jnp.dot(grad_up, up_full.T, preferred_element_type=jnp.float32)
        )
        back_two, ffn_piece = norm_back(hidden_one, inverse_two, ffn_gain, grad_normed_two)
        ffn_part = ffn_part + ffn_piece
        grad_hidden = grad_out + back_two
        grad_attn = gather_rows(grad_hidden.astype(jnp.bfloat16))
        out_acc = out_acc + jnp.dot(mixed_b.T, grad_attn, preferred_element_type=jnp.float32)
        grad_mixed = jnp.dot(grad_attn, out_full.T, preferred_element_type=jnp.float32).astype(
            jnp.bfloat16
        )
        grad_mixed = grad_mixed.reshape(seq_rows, kv_local, group_size, HD)
        scores = masked_scores(query_b, key_b, allowed, score_scale)
        attention = jnp.exp(scores - log_total)
        attention_b = attention.astype(jnp.bfloat16)
        grad_value = jnp.einsum(
            "ngqk,qngd->knd", attention_b, grad_mixed, preferred_element_type=jnp.float32
        )
        grad_attention = jnp.einsum(
            "qngd,knd->ngqk", grad_mixed, value_b, preferred_element_type=jnp.float32
        )
        grad_scores = attention * (
            grad_attention - jnp.sum(attention * grad_attention, axis=-1, keepdims=True)
        )
        grad_scores = grad_scores.astype(jnp.bfloat16)
        grad_query = (
            jnp.einsum("ngqk,knd->qngd", grad_scores, key_b, preferred_element_type=jnp.float32)
            * score_scale
        )
        grad_key = (
            jnp.einsum("ngqk,qngd->knd", grad_scores, query_b, preferred_element_type=jnp.float32)
            * score_scale
        )
        grad_qrot = rotary_back(grad_query.reshape(seq_rows, head_local, HD), cosine, sine_part)
        back_query, query_piece = norm_back(query_heads, inverse_q, query_gain, grad_qrot)
        grad_krot = rotary_back(grad_key, cosine, sine_part)
        back_key, key_piece = norm_back(key_heads, inverse_k, key_gain, grad_krot)
        query_part = query_part + query_piece
        key_part = key_part + key_piece
        grad_query_proj = back_query.reshape(seq_rows, head_local * HD).astype(jnp.bfloat16)
        grad_key_proj = back_key.reshape(seq_rows, kv_local * HD).astype(jnp.bfloat16)
        grad_value_proj = grad_value.reshape(seq_rows, kv_local * HD).astype(jnp.bfloat16)
        query_acc = query_acc + jnp.dot(
            gathered.T, grad_query_proj, preferred_element_type=jnp.float32
        )
        key_acc = key_acc + jnp.dot(gathered.T, grad_key_proj, preferred_element_type=jnp.float32)
        value_acc = value_acc + jnp.dot(
            gathered.T, grad_value_proj, preferred_element_type=jnp.float32
        )
        grad_normed = jnp.dot(grad_query_proj, query_full.T, preferred_element_type=jnp.float32)
        grad_normed = grad_normed + jnp.dot(
            grad_key_proj, key_full.T, preferred_element_type=jnp.float32
        )
        grad_normed = grad_normed + jnp.dot(
            grad_value_proj, value_full.T, preferred_element_type=jnp.float32
        )
        grad_normed = scatter_rows(grad_normed)
        back_one, attn_piece = norm_back(rows_in, inverse_one, attn_gain, grad_normed)
        attn_part = attn_part + attn_piece
        token_grads.append(grad_hidden + back_one)
    query_grad, key_grad, value_grad, out_grad, gate_grad, up_grad, down_grad = (
        lax.psum_scatter(
            query_acc.astype(jnp.bfloat16), "fsdp", scatter_dimension=0, tiled=True
        ).astype(jnp.float32),
        lax.psum_scatter(
            key_acc.astype(jnp.bfloat16), "fsdp", scatter_dimension=0, tiled=True
        ).astype(jnp.float32),
        lax.psum_scatter(
            value_acc.astype(jnp.bfloat16), "fsdp", scatter_dimension=0, tiled=True
        ).astype(jnp.float32),
        lax.psum_scatter(
            out_acc.astype(jnp.bfloat16), "fsdp", scatter_dimension=1, tiled=True
        ).astype(jnp.float32),
        lax.psum_scatter(
            gate_acc.astype(jnp.bfloat16), "fsdp", scatter_dimension=0, tiled=True
        ).astype(jnp.float32),
        lax.psum_scatter(
            up_acc.astype(jnp.bfloat16), "fsdp", scatter_dimension=0, tiled=True
        ).astype(jnp.float32),
        lax.psum_scatter(
            down_acc.astype(jnp.bfloat16), "fsdp", scatter_dimension=1, tiled=True
        ).astype(jnp.float32),
    )
    attn_total, query_total, key_total, ffn_total = lax.psum(
        (attn_part, query_part, key_part, ffn_part), ("fsdp", "tensor")
    )
    return (
        jnp.stack(outputs),
        jnp.stack(token_grads),
        attn_total,
        query_grad,
        key_grad,
        value_grad,
        query_total,
        key_total,
        out_grad,
        ffn_total,
        gate_grad,
        up_grad,
        down_grad,
    )


def swap_tensor(values):
    return lax.ppermute(values, "tensor", [(0, 1), (1, 0)])


def sequence_of(values, side):
    own = lax.dynamic_index_in_dim(values, side, 0, keepdims=False)
    other = swap_tensor(lax.dynamic_index_in_dim(values, 1 - side, 0, keepdims=False))
    first = jnp.where(side == 0, own, other)
    return jnp.concatenate([first, jnp.where(side == 0, other, own)], axis=0)


def rows_of(values, side, wire):
    halves = values.reshape((2, values.shape[0] // 2) + values.shape[1:])
    own = lax.dynamic_index_in_dim(halves, side, 0, keepdims=False)
    away = lax.dynamic_index_in_dim(halves, 1 - side, 0, keepdims=False)
    other = swap_tensor(away.astype(wire)).astype(values.dtype)
    return jnp.stack([jnp.where(side == 0, own, other), jnp.where(side == 0, other, own)])


def links():
    steps, distance = [("tensor", 1)], lax.axis_size("fsdp") // 2
    while distance:
        steps.append(("fsdp", distance))
        distance //= 2
    return steps


def exchange(values, link):
    name, distance = link
    pairs = [(i, i ^ distance) for i in range(lax.axis_size(name))]
    return lax.ppermute(values, name, pairs)


def total_of(values):
    for link in links():
        values = values + exchange(values, link)
    return values


def gather_steps(piece, order, steps):
    for step in order:
        other = exchange(piece, steps[step])
        piece = jnp.concatenate([piece, other], axis=step - 1 if step else piece.ndim - 1)
    return piece


def scatter_steps(values, order, steps):
    for step in order:
        axis = step - 1 if step else values.ndim - 1
        kept, sent = jnp.split(values, 2, axis=axis)
        other = exchange(sent, steps[step])
        values = (kept.astype(jnp.float32) + other.astype(jnp.float32)).astype(values.dtype)
    return values


def opened(weight, steps):
    return weight.reshape((1,) * (len(steps) - 1) + weight.shape)


def own_order(values, fsdp_index, blocks):
    grid = values.reshape(blocks, -1)
    return jnp.take(grid, jnp.arange(blocks) ^ fsdp_index, axis=0).reshape(values.shape)


def times(left, right):
    return jnp.dot(left, right, preferred_element_type=jnp.float32)


def times_t(left, right):
    return lax.dot_general(
        left, right, (((1,), (1,)), ((), ())), preferred_element_type=jnp.float32
    )


def rows_summed(left, right):
    return lax.dot_general(
        left, right, (((0,), (0,)), ((), ())), preferred_element_type=jnp.float32
    ).astype(jnp.bfloat16)


def whole_sequence(
    tokens,
    doc_lengths,
    attn_gain,
    query_weight,
    key_weight,
    value_weight,
    query_gain,
    key_gain,
    out_weight,
    ffn_gain,
    gate_weight,
    up_weight,
    down_weight,
    cotangent,
):
    side = lax.axis_index("tensor")
    blocks = lax.axis_size("fsdp")
    place = lax.axis_index("fsdp")
    q_cols = query_weight.shape[1]
    k_cols = key_weight.shape[1]
    group_size = H // KV
    score_scale = 1.0 / math.sqrt(HD)
    steps = links()
    last = len(steps) - 1
    far = list(range(1, last - 1))
    orders = (
        far + [last - 1, 0],
        far + [0, last - 1],
        [0, last - 1] + far,
    )
    qkv_local = jnp.concatenate([query_weight, key_weight, value_weight], axis=1)
    rows_own = sequence_of(tokens, side)
    qkv_part = gather_steps(opened(qkv_local, steps), orders[0], steps)
    out_part = gather_steps(opened(out_weight.T, steps), orders[1], steps)
    qkv_part, out_part, gate_local, up_local, down_local, cot_local = lax.optimization_barrier(
        (qkv_part, out_part, gate_weight, up_weight, down_weight, cotangent)
    )
    qkv_full = gather_steps(qkv_part, [last], steps).reshape(D, -1)
    out_full = gather_steps(out_part, [last], steps).reshape(D, -1)
    cot_own = sequence_of(cot_local, side)
    feed = [opened(weight, steps) for weight in (gate_local, up_local, down_local.T)]

    def grow(pieces, first, end=None):
        return [
            gather_steps(piece, order[first:end], steps) for piece, order in zip(pieces, orders)
        ]

    feed = grow(feed, 0, -2)
    features = jnp.arange(D)
    block_rows = D // blocks
    moved = ((features // block_rows) ^ place) * block_rows + features % block_rows
    order_mat = (moved[:, None] == features[None, :]).astype(jnp.bfloat16)
    rows_b = times(rows_own, order_mat).astype(jnp.bfloat16)
    cot_b = times(cot_own, order_mat).astype(jnp.bfloat16)
    attn_gain = own_order(attn_gain, place, blocks)
    ffn_gain = own_order(ffn_gain, place, blocks)
    seq_rows = rows_b.shape[0]
    lengths = lax.dynamic_index_in_dim(doc_lengths, side, 0, keepdims=False)[0]
    segment, offsets = position_tables(lengths, seq_rows)
    places = jnp.arange(seq_rows, dtype=jnp.int32)
    cosine, sine_part = rotary_tables(offsets, HD)
    allowed = (segment[:, None] == segment[None, :]) & (places[None, :] <= places[:, None])

    rows_in = rows_b.astype(jnp.float32)
    inverse_one = norm_stats(rows_in)
    normed_b = (rows_in * inverse_one * attn_gain).astype(jnp.bfloat16)
    v_at, one = q_cols + k_cols, q_cols + 2 * k_cols
    projected = times(normed_b, qkv_full)
    halves = (projected[:, :one], projected[:, one:])
    query_proj = jnp.concatenate([p[:, :q_cols] for p in halves], axis=1)
    key_proj = jnp.concatenate([p[:, q_cols:v_at] for p in halves], axis=1)
    value_proj = jnp.concatenate([p[:, v_at:] for p in halves], axis=1)
    query_heads = query_proj.reshape(seq_rows, H, HD)
    inverse_q = norm_stats(query_heads)
    query_b = rotary(query_heads * inverse_q * query_gain, cosine, sine_part).astype(jnp.bfloat16)
    query_b = query_b.reshape(seq_rows, KV, group_size, HD)
    key_heads = key_proj.reshape(seq_rows, KV, HD)
    inverse_k = norm_stats(key_heads)
    key_b = rotary(key_heads * inverse_k * key_gain, cosine, sine_part).astype(jnp.bfloat16)
    value_b = value_proj.reshape(seq_rows, KV, HD).astype(jnp.bfloat16)
    feed, query_b, key_b, value_b = lax.optimization_barrier((feed, query_b, key_b, value_b))
    feed = grow(feed, -2, -1)
    scores = masked_scores(query_b, key_b, allowed, score_scale)
    row_max = jnp.max(scores, axis=-1, keepdims=True)
    log_total = row_max + jnp.log(jnp.sum(jnp.exp(scores - row_max), axis=-1, keepdims=True))
    attention = jnp.exp(scores - log_total)
    attention_b = attention.astype(jnp.bfloat16)
    mixed_b = jnp.einsum("ngqk,knd->qngd", attention_b, value_b, preferred_element_type=jnp.float32)
    mixed_b = mixed_b.reshape(seq_rows, H * HD).astype(jnp.bfloat16)
    feed, mixed_b = lax.optimization_barrier((feed, mixed_b))
    feed = grow(feed, -1)
    hidden_one = rows_in + times_t(mixed_b, out_full)
    inverse_two = norm_stats(hidden_one)
    normed_two = (hidden_one * inverse_two * ffn_gain).astype(jnp.bfloat16)

    feed, normed_two = lax.optimization_barrier((feed, normed_two))
    gate_full, up_full, down_full = (
        gather_steps(piece, [last], steps).reshape(D, -1) for piece in feed
    )
    grad_out = cot_b.astype(jnp.float32)
    gate_act = times(normed_two, gate_full)
    up_act = times(normed_two, up_full)
    sig_gate = jax.nn.sigmoid(gate_act)
    inner_b = (gate_act * sig_gate * up_act).astype(jnp.bfloat16)
    grad_inner = times(cot_b, down_full)
    grad_gate = (grad_inner * up_act * sig_gate * (1.0 + gate_act * (1.0 - sig_gate))).astype(
        jnp.bfloat16
    )
    grad_up = (grad_inner * gate_act * sig_gate).astype(jnp.bfloat16)
    block_out = (hidden_one + times_t(inner_b, down_full)).astype(jnp.bfloat16)
    block_out = times(block_out, order_mat).astype(jnp.bfloat16)
    outputs = rows_of(block_out, side, jnp.bfloat16)
    wide = (blocks.bit_length() - 1) * (2,) + (block_rows, -1)

    def scatter_grad(grad, order):
        order = [last] + order[::-1]
        grad = scatter_steps(grad.reshape(wide), order, steps)
        return grad.reshape(block_rows, -1).astype(jnp.float32)

    def shrink(pieces, first, end=None):
        return [
            scatter_steps(piece, order[::-1][first:end], steps)
            for piece, order in zip(pieces, orders)
        ]

    feed_grads = [
        rows_summed(normed_two, grad_gate).reshape(wide),
        rows_summed(normed_two, grad_up).reshape(wide),
        rows_summed(cot_b, inner_b).reshape(wide),
    ]
    grad_normed_two = times_t(grad_gate, gate_full) + times_t(grad_up, up_full)
    feed_grads, grad_normed_two = lax.optimization_barrier((feed_grads, grad_normed_two))
    feed_grads = [scatter_steps(grad, [last], steps) for grad in feed_grads]

    back_two, ffn_part = norm_back(hidden_one, inverse_two, ffn_gain, grad_normed_two)
    grad_hidden = grad_out + back_two
    grad_attn = grad_hidden.astype(jnp.bfloat16)
    out_sum = rows_summed(grad_attn, mixed_b)
    grad_mixed = times(grad_attn, out_full).astype(jnp.bfloat16)
    feed_grads, out_sum, grad_mixed = lax.optimization_barrier((feed_grads, out_sum, grad_mixed))
    feed_grads = shrink(feed_grads, 0, 1)
    out_grad = scatter_grad(out_sum, orders[1])
    grad_mixed = grad_mixed.reshape(seq_rows, KV, group_size, HD)
    grad_value = jnp.einsum(
        "ngqk,qngd->knd", attention_b, grad_mixed, preferred_element_type=jnp.float32
    )
    grad_attention = jnp.einsum(
        "qngd,knd->ngqk", grad_mixed, value_b, preferred_element_type=jnp.float32
    )
    grad_scores = attention * (
        grad_attention - jnp.sum(attention * grad_attention, axis=-1, keepdims=True)
    )
    grad_scores = grad_scores.astype(jnp.bfloat16)
    feed_grads, grad_scores = lax.optimization_barrier((feed_grads, grad_scores))
    feed_grads = shrink(feed_grads, 1, 2)
    grad_query = (
        jnp.einsum("ngqk,knd->qngd", grad_scores, key_b, preferred_element_type=jnp.float32)
        * score_scale
    )
    grad_key = (
        jnp.einsum("ngqk,qngd->knd", grad_scores, query_b, preferred_element_type=jnp.float32)
        * score_scale
    )
    grad_qrot = rotary_back(grad_query.reshape(seq_rows, H, HD), cosine, sine_part)
    back_query, query_part = norm_back(query_heads, inverse_q, query_gain, grad_qrot)
    grad_krot = rotary_back(grad_key, cosine, sine_part)
    back_key, key_part = norm_back(key_heads, inverse_k, key_gain, grad_krot)
    grad_q = back_query.reshape(seq_rows, H * HD).astype(jnp.bfloat16)
    grad_k = back_key.reshape(seq_rows, KV * HD).astype(jnp.bfloat16)
    grad_v = grad_value.reshape(seq_rows, KV * HD).astype(jnp.bfloat16)
    grad_qkv = jnp.concatenate(
        [
            grad_q[:, :q_cols], grad_k[:, :k_cols], grad_v[:, :k_cols],
            grad_q[:, q_cols:], grad_k[:, k_cols:], grad_v[:, k_cols:],
        ],
        axis=1,
    )
    feed_grads, grad_qkv = lax.optimization_barrier((feed_grads, grad_qkv))
    gate_grad, up_grad, down_grad = (
        grad.reshape(block_rows, -1).astype(jnp.float32) for grad in shrink(feed_grads, 2)
    )
    qkv_grad = scatter_grad(rows_summed(normed_b, grad_qkv), orders[0])
    grad_normed = times_t(grad_qkv, qkv_full)
    back_one, attn_part = norm_back(rows_in, inverse_one, attn_gain, grad_normed)
    token_grad = grad_hidden + back_one
    high = token_grad.astype(jnp.bfloat16)
    low = (token_grad - high.astype(jnp.float32)).astype(jnp.bfloat16)
    token_grad = times(high, order_mat) + times(low, order_mat)
    token_grad = rows_of(token_grad, side, jnp.bfloat16)
    gain_parts = [
        own_order(attn_part, place, blocks), own_order(ffn_part, place, blocks),
        query_part, key_part,
    ]
    gain_total = total_of(jnp.concatenate(gain_parts))
    return (
        outputs,
        token_grad,
        gain_total[:D],
        qkv_grad[:, :q_cols],
        qkv_grad[:, q_cols:v_at],
        qkv_grad[:, v_at:],
        gain_total[2 * D : 2 * D + HD],
        gain_total[2 * D + HD :],
        out_grad.T,
        gain_total[D : 2 * D],
        gate_grad,
        up_grad,
        down_grad.T,
    )


def solution(mesh):
    fsdp, tensor = mesh.shape["fsdp"], mesh.shape["tensor"]
    run = on_device
    if tensor == MICRO == 2 and fsdp >= 8 and fsdp & (fsdp - 1) == 0:
        run = whole_sequence
    in_specs = (
        P(None, ("fsdp", "tensor"), None),
        P(None, "fsdp", None),
        P(),
        P("fsdp", "tensor"),
        P("fsdp", "tensor"),
        P("fsdp", "tensor"),
        P(),
        P(),
        P("tensor", "fsdp"),
        P(),
        P("fsdp", "tensor"),
        P("fsdp", "tensor"),
        P("tensor", "fsdp"),
        P(None, ("fsdp", "tensor"), None),
    )
    out_specs = (
        P(None, ("fsdp", "tensor"), None),
        P(None, ("fsdp", "tensor"), None),
        P(),
        P("fsdp", "tensor"),
        P("fsdp", "tensor"),
        P("fsdp", "tensor"),
        P(),
        P(),
        P("tensor", "fsdp"),
        P(),
        P("fsdp", "tensor"),
        P("fsdp", "tensor"),
        P("tensor", "fsdp"),
    )
    return jax.shard_map(
        run, mesh=mesh, in_specs=in_specs, out_specs=out_specs, check_vma=False
    )
```
